128 devices in a mesh: dp: 2 (over core), expert: 16 (over z, x), tensor: 4 (over y).
Axes of the slice: x: 4, y: 4, z: 4, core: 2. Of those that a mesh axis runs over, the one named last changes fastest.
Arguments:
- expert_out: bfloat16 [512, 16, 20, 7168], P(('dp', 'expert'), None, None, 'tensor'), parts along dimension 0, may hold values from -6 to 6
- expert_ids: int32 [16384, 8], P(('dp', 'expert')), parts along dimension 0, may hold values from 0 to 255, all different within a row; in each aligned block of 512 rows (0 to 511, 512 to 1023, ...) at most 20 rows name the same one
- gate_levels: int32 [16384, 8], P(('dp', 'expert')), parts along dimension 0, may hold values from 1 to 255
- residual: bfloat16 [16384, 7168], P(('dp', 'expert'), 'tensor'), parts along dimension 0, may hold values from -24 to 24
- attn_gain: float32 [7168], P('tensor'), may hold values from 0.1 to 1.9
- wq_a: bfloat16 [7168, 1536], P('tensor', 'expert'), may hold values from -0.0625 to 0.0625
- latent_gain: float32 [1536], replicated, may hold values from 0.1 to 1.9
- wq_b: bfloat16 [1536, 12288], P('expert', 'tensor'), may hold values from -0.15625 to 0.15625
Outputs:
- stream: bfloat16 [16384, 7168], P(('dp', 'expert'), 'tensor'), parts along dimension 0
- normed: bfloat16 [16384, 7168], P(('dp', 'expert'), 'tensor'), parts along dimension 0
- queries: bfloat16 [16384, 12288], P(('dp', 'expert'), 'tensor'), parts along dimension 0
The draws below stay inside these ranges and needn't reach their ends.
There are 2 independent parts, one for each index of `dp`. The reference program is written for one: setup_inputs(seed, part) draws one part's arguments, and reference() takes and returns one part's arrays. A program takes and returns all parts, laid end to end along the dimension named above; an argument that names none is the same for every part. Nothing has to cross between parts.
Inputs may be any that keep to these rules, and one draw needn't show every extreme that they name: `expert_ids`: each row names 8 different experts. Among the 512 rows of one owner (aligned blocks of rows) no expert is named more than 20 times, a bound that some block reaches.
All inputs are finite; a program needn't handle non-finite values.
Results may differ from the reference program's by a relative error of at most 0.024.
Values may be sent and summed in bfloat16 or wider, within the bound.
No kernel may reach another device: no remote copies, remote signals or barrier semaphores. Data moves between devices by JAX's collectives and lax.ppermute only.
A program may use at most 192 MiB of HBM per device.

```python
import math
import jax
import jax.numpy as jnp
import numpy as np
from jax import lax

D = 7168
QL = 1536
HEADS = 64
DH = 192
TOP = 8
EXP_DEV = 16
TOK_DEV = 512
EXPERTS = 256
CAP = 20
TOKENS = 8192
N_EXPERT = 16


def draw_residual(key, part):
    key = jax.random.fold_in(key, 11)
    first, second, third = jax.random.split(key, 3)
    base = jax.random.normal(first, (TOKENS, D), jnp.float32)
    column = jnp.arange(D, dtype=jnp.float32) / D
    row_scale = 10.0 ** jax.random.uniform(second, (TOKENS, 1), jnp.float32, -0.5, 0.5)
    col_scale = 3.0 ** (column - 0.5) * 10.0 ** jax.random.uniform(third, (D,), jnp.float32, -0.3, 0.3)
    values = row_scale * base * col_scale[None, :]
    return jnp.clip(values, -24.0, 24.0).astype(jnp.bfloat16)


def place_ends(drawn, key, low, top_value):
    longest = drawn.shape.index(max(drawn.shape))
    spots = []
    for shift in (0, 1):
        where = [jax.random.randint(jax.random.fold_in(key, axis), (), 0, length) for axis, length in enumerate(drawn.shape)]
        where[longest] = (where[longest] + shift) % drawn.shape[longest]
        spots.append(tuple(where))
    return drawn.at[spots[0]].set(low).at[spots[1]].set(top_value)


def level_of(rng, dims, cuts, smallest, top_value):
    loudness, own = 1.0, jax.random.fold_in(rng, 6)
    for dim, parts in cuts:
        draws = jnp.exp(jax.random.uniform(jax.random.fold_in(own, dim), (parts,), jnp.float32, smallest / len(cuts), top_value / len(cuts)))
        loudness = loudness * jnp.repeat(draws, dims[dim] // parts).reshape([-1 if axis == dim else 1 for axis in range(len(dims))])
    return loudness


def assign_block(stream_key, own, number, rows, amount, top, reach, slope):
    sequence = jax.random.permutation(stream_key, amount)
    packed, common = shares(amount, rows * top, reach, slope, True), shares(amount, rows * top, reach, slope, False)
    places = jnp.arange(amount)

    def named(sizes, turn):
        used = int((sizes > 0).sum())
        fixed = max(1, used // 4)
        passed = fixed + (places - fixed + turn * (used - fixed)) % max(1, amount - fixed)
        return jnp.zeros((amount,), jnp.int32).at[sequence[jnp.where(places < fixed, places, passed)]].set(jnp.asarray(sizes, jnp.int32))

    sizes = jnp.where(number % 4 == 0, named(packed, number // 4), named(common, number - number // 4 - 1))
    mixed = jax.random.permutation(jax.random.fold_in(own, 3), amount)
    giver, taker = mixed[0:amount // 2 * 2:2], mixed[1:amount // 2 * 2:2]
    margin = jnp.minimum(sizes[giver] - 1, reach - sizes[taker]) // 2
    margin = jnp.where((giver == sequence[0]) | (taker == sequence[0]) | (sizes[taker] == 0), 0, jnp.maximum(margin, 0))
    passed = jax.random.randint(jax.random.fold_in(own, 4), (amount // 2,), 0, 1 << 20) % (margin + 1)
    sizes = sizes.at[giver].add(-passed).at[taker].add(passed)
    members = jnp.searchsorted(jnp.cumsum(sizes), jnp.arange(rows * top), side="right").astype(jnp.int32)
    listing = members.reshape(top, rows).T
    listing = listing[jax.random.permutation(jax.random.fold_in(own, 1), rows)]
    turn = jax.random.randint(jax.random.fold_in(own, 2), (rows, 1), 0, top)
    return jnp.take_along_axis(listing, (jnp.arange(top)[None, :] + turn) % top, axis=1)


def shares(number_of, total, limit, slope, full):
    portions = [(1 << 20) // math.isqrt(standing ** slope) + 1 for standing in range(1, number_of + 1)]
    largest = limit if full else min(limit, max(-(-total // number_of), total * portions[0] // sum(portions)))
    least = 1 if total - largest >= number_of - 1 else 0
    counts, surplus = [largest] + [least] * (number_of - 1), total - largest - least * (number_of - 1)
    while surplus > 0:
        candidates = [i for i in range(1, number_of) if counts[i] < largest] or [i for i in range(1, number_of) if counts[i] < limit]
        mass, left = sum([portions[i] for i in candidates]), surplus
        for i in candidates:
            addition = min(limit - counts[i], max(1, left * portions[i] // mass), surplus)
            counts[i] = counts[i] + addition
            surplus = surplus - addition
    return np.array(counts)


def gaussian(own_key, dims, deviation, limit, pieces=(), kind=jnp.bfloat16):
    loudness = level_of(own_key, dims, pieces, -0.22, 0.18) if pieces else 1.0
    array = jax.random.normal(own_key, dims, jnp.float32) * deviation * loudness
    return jnp.minimum(jnp.maximum(array, -limit), limit).astype(kind)


def setup_inputs(seed: int = 0, part: int = 0) -> dict:
    key_of = jax.random.split(jax.random.key(seed), 9)
    part_keys = jax.random.split(jax.random.fold_in(key_of[8], part), 9)
    expert_out = gaussian(part_keys[0], (EXPERTS, N_EXPERT, CAP, D), 1.0, 6.0, ((0, 16), (3, 4)))
    expert_ids_keys = jax.random.split(jax.random.fold_in(part_keys[1], 1), TOKENS // TOK_DEV)
    expert_ids_turns = jax.random.permutation(jax.random.fold_in(part_keys[1], 3), TOKENS // TOK_DEV)
    expert_ids = jax.vmap(lambda own, number: assign_block(jax.random.fold_in(part_keys[1], 2), own, number, TOK_DEV, EXPERTS, TOP, CAP, 2))(expert_ids_keys, expert_ids_turns).reshape((TOKENS, TOP))
    gate_levels = place_ends(jax.random.randint(part_keys[2], (TOKENS, TOP), 1, 256), jax.random.fold_in(part_keys[2], 1), 1, 255).astype(jnp.int32)
    residual = draw_residual(jax.random.fold_in(jax.random.fold_in(key_of[8], part), 71), part)
    attn_gain = jnp.clip(1.0 + 0.18 * jax.random.normal(key_of[4], (D,), jnp.float32), 0.1, 1.9)
    wq_a = gaussian(key_of[5], (D, QL), D ** -0.5, 0.0625, ((0, 4), (1, 16)))
    latent_gain = jnp.clip(1.0 + 0.18 * jax.random.normal(key_of[6], (QL,), jnp.float32), 0.1, 1.9)
    wq_b = gaussian(key_of[7], (QL, HEADS * DH), QL ** -0.5, 0.15625, ((0, 16), (1, 4)))
    return dict(expert_out=expert_out, expert_ids=expert_ids, gate_levels=gate_levels, residual=residual, attn_gain=attn_gain, wq_a=wq_a, latent_gain=latent_gain, wq_b=wq_b)


route_scale = 2.5
epsilon = 1e-06

def block_ranks(owner_ids, expert_total):
    length = owner_ids.shape[0]
    one_hot = lax.optimization_barrier(jnp.sum((owner_ids[:, :, None] == jnp.arange(expert_total, dtype=jnp.int32)[None, None, :]).astype(jnp.float32), axis=1))
    position = jnp.arange(length, dtype=jnp.int32)
    earlier = (position[:, None] > position[None, :]).astype(jnp.float32)
    before = jnp.dot(earlier, one_hot, precision=lax.Precision.HIGHEST, preferred_element_type=jnp.float32)
    return jnp.take_along_axis(before, owner_ids, axis=1).astype(jnp.int32)

def gate_weights(levels):
    wide = levels.astype(jnp.float32)
    return route_scale * wide / lax.optimization_barrier(jnp.sum(wide, axis=1, keepdims=True))

def reference(expert_out, expert_ids, gate_levels, residual, attn_gain, wq_a, latent_gain, wq_b):
    owner_ids = expert_ids.reshape(N_EXPERT, TOK_DEV, TOP)
    owner_levels = gate_levels.reshape(N_EXPERT, TOK_DEV, TOP)

    def one_owner(bundle):
        owner, block_ids, block_levels = bundle
        slot_rank = block_ranks(block_ids, EXPERTS)
        weight = gate_weights(block_levels)
        picked = expert_out[block_ids, owner, slot_rank].astype(jnp.float32) * weight[:, :, None]
        holder = block_ids // EXP_DEV
        holder_hot = (holder[:, :, None] == jnp.arange(N_EXPERT, dtype=jnp.int32)[None, None, :]).astype(jnp.float32)
        holder_sum = jnp.einsum('tkd,tkh->thd', picked, holder_hot)
        rounded = lax.optimization_barrier(holder_sum.astype(jnp.bfloat16)).astype(jnp.float32)
        return lax.optimization_barrier(jnp.sum(rounded, axis=1))
    combined = lax.map(one_owner, (jnp.arange(N_EXPERT, dtype=jnp.int32), owner_ids, owner_levels)).reshape(TOKENS, D)
    stream = (residual.astype(jnp.float32) + combined).astype(jnp.bfloat16)
    stream_wide = stream.astype(jnp.float32)
    inv_scale = lax.rsqrt(lax.optimization_barrier(jnp.sum(stream_wide * stream_wide, axis=1)) / D + epsilon)
    normed = (stream_wide * inv_scale[:, None] * attn_gain).astype(jnp.bfloat16)
    latent = jnp.dot(normed, wq_a, preferred_element_type=jnp.float32)
    latent_scale = lax.rsqrt(lax.optimization_barrier(jnp.sum(latent * latent, axis=1)) / QL + epsilon)
    compressed = (latent * latent_scale[:, None] * latent_gain).astype(jnp.bfloat16)
    queries = jnp.dot(compressed, wq_b, preferred_element_type=jnp.float32).astype(jnp.bfloat16)
    return (stream, normed, queries)
```

```python
import jax
import jax.numpy as jnp
import numpy as np
from jax import lax
from jax.experimental import pallas as pl
from jax.experimental.pallas import tpu as pltpu
from jax.sharding import PartitionSpec as P

D = 7168
QL = 1536
CAP = 20
HOLD = 16
SLOTS = HOLD * CAP
SIDE = 4
RING = 16
ROUTE_SCALE = 2.5
EPSILON = 1e-06

GROUPS = ((0, 512), (512, 512), (1024, 384), (1408, 384))
ORDERS = ("PQpq", "QpqP", "pqPQ", "qPQp")
EVEN = (1, 0, 3, 2)
ODD = (3, 2, 1, 0)


def partner(kind, place):
    slow, fast = divmod(place, SIDE)
    if kind == "P":
        slow = EVEN[slow]
    elif kind == "Q":
        slow = ODD[slow]
    elif kind == "p":
        fast = EVEN[fast]
    else:
        fast = ODD[fast]
    return slow * SIDE + fast


def order_of(group, half):
    return ORDERS[(group + 2 * half) % 4]


def keep(order, step, place):
    if step == 4:
        return [place]
    return keep(order, step + 1, partner(order[step], place)) + keep(order, step + 1, place)


def owner_table():
    return np.array(
        [[[keep(order_of(g, h), 0, e) for g in range(4)] for e in range(RING)] for h in range(2)],
        np.int32,
    )


def holder_table():
    return np.array(
        [[[e] + [partner(order_of(g, h)[0], e) for g in range(4)] for e in range(RING)] for h in range(2)],
        np.int32,
    )


def swap(value, group, step):
    pairs = [
        (half * RING + e, half * RING + partner(order_of(group, half)[step], e))
        for half in range(2)
        for e in range(RING)
    ]
    return lax.ppermute(value, ("dp", "expert"), pairs)


def relay_kernel(owner_ref, x_ref, first_ref, second_ref, keep_ref, turned):
    turned[...] = jnp.swapaxes(x_ref[...], 0, 1)
    for i in range(4):
        first_ref[i] = turned[owner_ref[i]]
        second_ref[i] = turned[owner_ref[4 + i]]
    for i in range(8):
        keep_ref[i] = turned[owner_ref[8 + i]]


def relay(slots, owners, start, width):
    lanes = 128
    base = start // lanes
    out = lambda n: pl.BlockSpec((n, SLOTS, lanes), lambda j, o: (0, 0, j))
    return pl.pallas_call(
        relay_kernel,
        grid_spec=pltpu.PrefetchScalarGridSpec(
            num_scalar_prefetch=1,
            grid=(width // lanes,),
            in_specs=[pl.BlockSpec((SLOTS, RING, lanes), lambda j, o: (0, 0, base + j))],
            out_specs=[out(4), out(4), out(8)],
            scratch_shapes=[pltpu.VMEM((RING, SLOTS, lanes), jnp.bfloat16)],
        ),
        out_shape=[
            jax.ShapeDtypeStruct((n, SLOTS, width), jnp.bfloat16) for n in (4, 4, 8)
        ],
        compiler_params=pltpu.CompilerParams(vmem_limit_bytes=40 << 20),
        cost_estimate=pl.CostEstimate(
            flops=0, bytes_accessed=2 * RING * SLOTS * width * 2, transcendentals=0
        ),
        name="relay",
    )(owners, slots)


def route_kernel(packed_ref, expert_ref, earlier_ref, out_ref):
    table = packed_ref[0].astype(jnp.float32).T
    levels = table[:, 8:16]
    weight = ROUTE_SCALE * levels / jnp.sum(levels, axis=1, keepdims=True)
    experts = expert_ref[0:1, :]
    named = jnp.zeros((table.shape[0], 128), jnp.float32)
    weighed = jnp.zeros((table.shape[0], 128), jnp.float32)
    for k in range(8):
        hit = table[:, k : k + 1] == experts
        named = jnp.where(hit, 1.0, named)
        weighed = jnp.where(hit, weight[:, k : k + 1], weighed)
    rank = jnp.dot(earlier_ref[...], named.astype(jnp.bfloat16), preferred_element_type=jnp.float32)
    out_ref[0, :, 0:128] = weighed.astype(jnp.bfloat16)
    out_ref[0, :, 128:256] = rank.astype(jnp.bfloat16)


def route(packed, experts, earlier, tokens):
    return pl.pallas_call(
        route_kernel,
        grid=(RING,),
        in_specs=[
            pl.BlockSpec((1, 16, tokens), lambda i: (i, 0, 0)),
            pl.BlockSpec((8, 128), lambda i: (0, 0)),
            pl.BlockSpec((tokens, tokens), lambda i: (0, 0)),
        ],
        out_specs=pl.BlockSpec((1, tokens, 256), lambda i: (i, 0, 0)),
        out_shape=jax.ShapeDtypeStruct((RING, tokens, 256), jnp.bfloat16),
        compiler_params=pltpu.CompilerParams(vmem_limit_bytes=40 << 20),
        cost_estimate=pl.CostEstimate(
            flops=RING * 2 * tokens * tokens * 128 * 4, bytes_accessed=RING * tokens * 512, transcendentals=0
        ),
        name="route",
    )(packed, experts, earlier)


def combine_kernel(owner_ref, route_ref, spread_ref, turn_ref, mine_ref, theirs_ref, out_ref, rows):
    rows[0:SLOTS] = mine_ref[0]
    rows[SLOTS : 2 * SLOTS] = theirs_ref[0]
    weight = jnp.dot(route_ref[0, :, 0:128], spread_ref[...], preferred_element_type=jnp.float32)
    rank = jnp.dot(route_ref[0, :, 128:256], spread_ref[...], preferred_element_type=jnp.float32)
    matrix = jnp.where(rank == turn_ref[0:1, :], weight, 0.0).astype(jnp.bfloat16)
    out_ref[0] = jnp.dot(matrix, rows[...], preferred_element_type=jnp.float32).astype(jnp.bfloat16)


def combine(owners, routes, spread, turn, mine, theirs, first, count, tokens):
    width = mine.shape[2]
    return pl.pallas_call(
        combine_kernel,
        grid_spec=pltpu.PrefetchScalarGridSpec(
            num_scalar_prefetch=1,
            grid=(count,),
            in_specs=[
                pl.BlockSpec((1, tokens, 256), lambda i, o: (o[8 + first + i], 0, 0)),
                pl.BlockSpec((128, 2 * SLOTS), lambda i, o: (0, 0)),
                pl.BlockSpec((8, 2 * SLOTS), lambda i, o: (0, 0)),
                pl.BlockSpec((1, SLOTS, width), lambda i, o: (first + i, 0, 0)),
                pl.BlockSpec((1, SLOTS, width), lambda i, o: (first % 4 + i, 0, 0)),
            ],
            out_specs=pl.BlockSpec((1, tokens, width), lambda i, o: (i, 0, 0)),
            scratch_shapes=[pltpu.VMEM((2 * SLOTS, width), jnp.bfloat16)],
        ),
        out_shape=jax.ShapeDtypeStruct((count, tokens, width), jnp.bfloat16),
        compiler_params=pltpu.CompilerParams(vmem_limit_bytes=40 << 20),
        cost_estimate=pl.CostEstimate(
            flops=count * 2 * tokens * 2 * SLOTS * (width + 256),
            bytes_accessed=count * (tokens * width + 2 * SLOTS * width + tokens * 256) * 2,
            transcendentals=0,
        ),
        name="combine",
    )(owners, routes, spread, turn, mine, theirs)


def wide(value):
    return value.astype(jnp.float32)


def shards(expert_out, expert_ids, gate_levels, residual, attn_gain, wq_a, latent_gain, wq_b):
    half = lax.axis_index("dp")
    place = lax.axis_index("expert")
    lane = lax.axis_index("tensor")
    tokens = expert_ids.shape[0]
    columns = residual.shape[1]

    owners = jnp.asarray(owner_table())[half, place]
    holders = jnp.asarray(holder_table())[half, place]
    experts = (holders[:, None] * HOLD + jnp.arange(HOLD, dtype=jnp.int32)[None, :]).reshape(-1)
    experts = jnp.concatenate([experts, jnp.full((128 - experts.shape[0],), -1, jnp.int32)])
    experts = jnp.broadcast_to(experts.astype(jnp.float32)[None, :], (8, 128))

    packed = jnp.concatenate([expert_ids.T, gate_levels.T], axis=0)
    packed = lax.all_gather(packed, "expert", axis=0)

    part = wq_b.shape[0] // 2
    down_mine = lax.dynamic_slice_in_dim(wq_a.T, half * part, part, 0)
    up_mine = lax.dynamic_slice_in_dim(wq_b, half * part, part, 0)
    down_mine = lax.all_gather(down_mine, "expert", axis=0, tiled=True)
    up_mine = lax.all_gather(up_mine, "expert", axis=0, tiled=True)
    other = [(0, 1), (1, 0)]
    down_theirs = lax.ppermute(down_mine, "dp", other)
    up_theirs = lax.ppermute(up_mine, "dp", other)
    gain = latent_gain.reshape(RING, 2, part).transpose(1, 0, 2)
    gain = jnp.concatenate([gain[half], gain[1 - half]], axis=0).reshape(-1)

    slots = expert_out.transpose(0, 2, 1, 3).reshape(SLOTS, RING, columns)
    relayed = [relay(slots, owners[g], *GROUPS[g]) for g in range(4)]
    first = [[swap(relayed[g][i], g, 0) for g in range(4)] for i in range(2)]

    position = jnp.arange(tokens, dtype=jnp.int32)
    earlier = (position[:, None] > position[None, :]).astype(jnp.bfloat16)
    routes = route(packed, experts, earlier, tokens)
    slot = np.arange(SLOTS)
    turn = jnp.asarray(np.broadcast_to(np.tile(slot % CAP, 2)[None, :], (8, 2 * SLOTS)).astype(np.float32))
    lanes = np.arange(128)[:, None]
    spread = [
        jnp.asarray(
            np.concatenate(
                [lanes == (slot // CAP)[None, :], lanes == (slot // CAP)[None, :] + HOLD * (g + 1)], axis=1
            ).astype(np.float32)
        ).astype(jnp.bfloat16)
        for g in range(4)
    ]

    def summed(g, start, received):
        return combine(owners[g], routes, spread[g], turn, relayed[g][2], received, start, 2, tokens)

    pass_a = [summed(g, 0, first[0][g]) for g in range(4)]
    second_a = [swap(pass_a[g], g, 1) for g in range(4)]
    pass_b = [summed(g, 2, first[0][g]) for g in range(4)]
    second_b = [swap(pass_b[g], g, 1) for g in range(4)]
    kept_a = [summed(g, 4, first[1][g]) for g in range(4)]
    kept_b = [summed(g, 6, first[1][g]) for g in range(4)]
    third = [
        swap((wide(kept_a[g]) + wide(second_a[g])).astype(jnp.bfloat16), g, 2) for g in range(4)
    ]
    fourth = [
        swap(
            (wide(kept_b[g][0]) + wide(second_b[g][0]) + wide(third[g][0])).astype(jnp.bfloat16), g, 3
        )
        for g in range(4)
    ]
    combined = jnp.concatenate(
        [
            wide(kept_b[g][1]) + wide(second_b[g][1]) + wide(third[g][1]) + wide(fourth[g])
            for g in range(4)
        ],
        axis=1,
    )
    stream = (wide(residual) + combined).astype(jnp.bfloat16)
    stream_wide = wide(stream)
    squares = lax.psum(jnp.sum(stream_wide * stream_wide, axis=1), "tensor")
    scaled = (stream_wide * attn_gain).astype(jnp.bfloat16)
    over_rows = (((1,), (1,)), ((), ()))
    latent = jnp.concatenate(
        [
            lax.dot_general(scaled, weights, over_rows, preferred_element_type=jnp.float32)
            for weights in (down_mine, down_theirs)
        ],
        axis=1,
    ).astype(jnp.bfloat16)
    count = lax.axis_size("tensor")
    rows = tokens // count
    latent = latent.reshape(count, rows, QL)

    def turned(value, shift):
        return lax.ppermute(value, "tensor", [(y, (y + shift) % count) for y in range(count)])

    total = wide(lax.dynamic_index_in_dim(latent, lane, 0, keepdims=False))
    for shift in (2, 1, 3):
        piece = lax.dynamic_index_in_dim(latent, (lane + shift) % count, 0, keepdims=False)
        total = total + wide(turned(piece, shift))
    inv_scale = lax.rsqrt(squares / D + EPSILON)
    normed = (stream_wide * inv_scale[:, None] * attn_gain).astype(jnp.bfloat16)
    total = total * lax.dynamic_slice_in_dim(inv_scale, lane * rows, rows, 0)[:, None]
    latent_scale = lax.rsqrt(jnp.sum(total * total, axis=1) / QL + EPSILON)
    compressed = (total * latent_scale[:, None] * gain).astype(jnp.bfloat16)
    everyone = jnp.zeros((count, rows, QL), jnp.bfloat16)
    everyone = lax.dynamic_update_index_in_dim(everyone, compressed, lane, 0)
    for shift in (2, 1, 3):
        everyone = lax.dynamic_update_index_in_dim(
            everyone, turned(compressed, shift), (lane - shift) % count, 0
        )
    everyone = everyone.reshape(tokens, QL)
    middle = QL // 2
    queries = jnp.dot(everyone[:, :middle], up_mine, preferred_element_type=jnp.float32) + jnp.dot(
        everyone[:, middle:], up_theirs, preferred_element_type=jnp.float32
    )
    return (stream, normed, queries.astype(jnp.bfloat16))


def solution(mesh):
    return jax.shard_map(
        shards,
        mesh=mesh,
        in_specs=(
            P(("dp", "expert"), None, None, "tensor"),
            P(("dp", "expert"), None),
            P(("dp", "expert"), None),
            P(("dp", "expert"), "tensor"),
            P("tensor"),
            P("tensor", "expert"),
            P(),
            P("expert", "tensor"),
        ),
        out_specs=(
            P(("dp", "expert"), "tensor"),
            P(("dp", "expert"), "tensor"),
            P(("dp", "expert"), "tensor"),
        ),
        check_vma=False,
    )
```

```python
import functools

import jax
import jax.numpy as jnp
import numpy as np
from jax import lax
from jax.experimental import pallas as pl
from jax.experimental.pallas import tpu as pltpu
from jax.sharding import PartitionSpec as P

D = 7168
QL = 1536
CAP = 20
HOLD = 16
SLOTS = HOLD * CAP
SIDE = 4
RING = 16
ROUTE_SCALE = 2.5
EPSILON = 1e-06
STEP = 4.0
VMEM = 60 << 20

ORDERS = ("PQpq", "QpqP", "pqPQ", "qPQp")
GROUPS = 2
EVEN = (1, 0, 3, 2)
ODD = (3, 2, 1, 0)


def partner(kind, place):
    slow, fast = divmod(place, SIDE)
    if kind == "P":
        slow = EVEN[slow]
    elif kind == "Q":
        slow = ODD[slow]
    elif kind == "p":
        fast = EVEN[fast]
    else:
        fast = ODD[fast]
    return slow * SIDE + fast


def order_of(group, half):
    return ORDERS[2 * group + half]


def keep(order, step, place):
    if step == 4:
        return [place]
    return keep(order, step + 1, partner(order[step], place)) + keep(order, step + 1, place)


def owner_table():
    return np.array(
        [[[keep(order_of(g, h), 0, e) for g in range(GROUPS)] for e in range(RING)] for h in range(2)],
        np.int32,
    )


def holder_table():
    return np.array(
        [
            [[e] + [partner(order_of(g, h)[0], e) for g in range(GROUPS)] for e in range(RING)]
            for h in range(2)
        ],
        np.int32,
    )


def gathered(place, steps):
    if not steps:
        return [place]
    return gathered(place, steps[:-1]) + gathered(partner(steps[-1], place), steps[:-1])


def spot_table():
    places = [gathered(e, ORDERS[0]) for e in range(RING)]
    owners = owner_table()
    return np.array(
        [
            [[[places[e].index(o) for o in owners[h, e, g]] for g in range(GROUPS)] for e in range(RING)]
            for h in range(2)
        ],
        np.int32,
    )


def swap(value, group, step):
    pairs = [
        (half * RING + e, half * RING + partner(order_of(group, half)[step], e))
        for half in range(2)
        for e in range(RING)
    ]
    return lax.ppermute(value, ("dp", "expert"), pairs)


RING_STEPS = ((EVEN, ODD), (ODD, EVEN))
QUARTERS = np.array([[0, 2, 3, 1], [0, 1, 2, 3]], np.int32)


def turn_to(value, step):
    pairs = [(h * 4 + y, h * 4 + RING_STEPS[h][step][y]) for h in range(2) for y in range(4)]
    return lax.ppermute(value, ("dp", "tensor"), pairs)


def relay_kernel(move_ref, x_ref, first_ref, second_ref, keep_ref):
    for b in range(x_ref.shape[0] // RING):
        rows = slice(b * RING, (b + 1) * RING)
        block = x_ref[rows].reshape(RING * RING, x_ref.shape[2])
        moved = jnp.dot(move_ref[...], block, preferred_element_type=jnp.float32).astype(jnp.bfloat16)
        moved = moved.reshape(RING, RING, x_ref.shape[2])
        first_ref[:, rows] = moved[0:4]
        second_ref[:, rows] = moved[4:8]
        keep_ref[:, rows] = moved[8:16]


def relay(slots, move, group):
    width = slots.shape[2] // GROUPS
    rows = SLOTS // 2
    out = lambda n: pl.BlockSpec((n, rows, width), lambda i: (0, i, 0))
    return pl.pallas_call(
        relay_kernel,
        grid=(SLOTS // rows,),
        in_specs=[
            pl.BlockSpec((RING * RING, RING * RING), lambda i: (0, 0)),
            pl.BlockSpec((rows, RING, width), lambda i: (i, 0, group)),
        ],
        out_specs=[out(4), out(4), out(8)],
        out_shape=[jax.ShapeDtypeStruct((n, SLOTS, width), jnp.bfloat16) for n in (4, 4, 8)],
        compiler_params=pltpu.CompilerParams(vmem_limit_bytes=VMEM),
        cost_estimate=pl.CostEstimate(
            flops=2 * RING * SLOTS * RING * RING * width,
            bytes_accessed=4 * RING * SLOTS * width,
            transcendentals=0,
        ),
        name="relay",
    )(move, slots)


def route_kernel(packed_ref, expert_ref, later_ref, out_ref):
    tokens = packed_ref.shape[2]
    rows = expert_ref.shape[0]
    experts = expert_ref[...]
    for i in range(packed_ref.shape[0]):
        table = packed_ref[i].astype(jnp.float32)
        levels = table[8:16]
        weight = ROUTE_SCALE * levels / jnp.sum(levels, axis=0, keepdims=True)
        named = jnp.zeros((rows, tokens), jnp.float32)
        weighed = jnp.zeros((rows, tokens), jnp.float32)
        for k in range(8):
            hit = experts == table[k : k + 1]
            named = jnp.where(hit, 1.0, named)
            weighed = jnp.where(hit, weight[k : k + 1], weighed)
        rank = jnp.dot(named.astype(jnp.bfloat16), later_ref[...], preferred_element_type=jnp.float32)
        out_ref[i] = jnp.concatenate([weighed, rank], axis=0).T.astype(jnp.bfloat16)


def route(packed, experts, later, tokens):
    rows = experts.shape[0]
    count = 8
    return pl.pallas_call(
        route_kernel,
        grid=(RING // count,),
        in_specs=[
            pl.BlockSpec((count, 16, tokens), lambda i: (i, 0, 0)),
            pl.BlockSpec((rows, tokens), lambda i: (0, 0)),
            pl.BlockSpec((tokens, tokens), lambda i: (0, 0)),
        ],
        out_specs=pl.BlockSpec((count, tokens, 2 * rows), lambda i: (i, 0, 0)),
        out_shape=jax.ShapeDtypeStruct((RING, tokens, 2 * rows), jnp.bfloat16),
        compiler_params=pltpu.CompilerParams(vmem_limit_bytes=VMEM),
        cost_estimate=pl.CostEstimate(
            flops=RING * 2 * tokens * tokens * 256, bytes_accessed=RING * tokens * 256, transcendentals=0
        ),
        name="route",
    )(packed, experts, later)


def combine_kernel(spot_ref, route_ref, spread_ref, turn_ref, mine_ref, theirs_ref, *rest, outs):
    rows = rest[-1]
    rows[0:SLOTS] = mine_ref[0]
    rows[SLOTS : 2 * SLOTS] = theirs_ref[0]
    level = jnp.dot(route_ref[0], spread_ref[...], preferred_element_type=jnp.float32) - turn_ref[0:1, :]
    matrix = jnp.where(jnp.abs(level - 1.25) < 1.5, level, 0.0).astype(jnp.bfloat16)
    value = jnp.dot(matrix, rows[...], preferred_element_type=jnp.float32)
    if len(rest) > 1 + outs:
        value += wide(rest[0][0])
    value = value.astype(jnp.bfloat16)
    if outs == 1:
        rest[-2][0] = value
    else:
        for i in range(outs):

            @pl.when(pl.program_id(0) == i)
            def _():
                rest[i - 1 - outs][...] = value


def combine(spots, routes, spread, turn, mine, theirs, first, count, tokens, more=()):
    width = mine.shape[2]
    lanes = routes.shape[2]
    outs = count if more else 1
    if more:
        out_specs = [pl.BlockSpec((tokens, width), lambda i, o: (0, 0))] * count
        out_shape = [jax.ShapeDtypeStruct((tokens, width), jnp.bfloat16)] * count
    else:
        out_specs = pl.BlockSpec((1, tokens, width), lambda i, o: (i, 0, 0))
        out_shape = jax.ShapeDtypeStruct((count, tokens, width), jnp.bfloat16)
    return pl.pallas_call(
        functools.partial(combine_kernel, outs=outs),
        grid_spec=pltpu.PrefetchScalarGridSpec(
            num_scalar_prefetch=1,
            grid=(count,),
            in_specs=[
                pl.BlockSpec((1, tokens, lanes), lambda i, o: (o[8 + first + i], 0, 0)),
                pl.BlockSpec((lanes, 2 * SLOTS), lambda i, o: (0, 0)),
                pl.BlockSpec((8, 2 * SLOTS), lambda i, o: (0, 0)),
                pl.BlockSpec((1, SLOTS, width), lambda i, o: (first + i, 0, 0)),
                pl.BlockSpec((1, SLOTS, width), lambda i, o: (first % 4 + i, 0, 0)),
            ]
            + [pl.BlockSpec((1, tokens, width), lambda i, o: (i, 0, 0))] * len(more),
            out_specs=out_specs,
            scratch_shapes=[pltpu.VMEM((2 * SLOTS, width), jnp.bfloat16)],
        ),
        out_shape=out_shape,
        compiler_params=pltpu.CompilerParams(vmem_limit_bytes=VMEM),
        cost_estimate=pl.CostEstimate(
            flops=count * 2 * tokens * 2 * SLOTS * (width + 256),
            bytes_accessed=count * (tokens * width + 2 * SLOTS * width + tokens * lanes) * 2,
            transcendentals=0,
        ),
        name="combine",
    )(spots, routes, spread, turn, mine, theirs, *more)


def add_kernel(left_ref, right_ref, out_ref):
    out_ref[...] = (wide(left_ref[...]) + wide(right_ref[...])).astype(jnp.bfloat16)


def add(left, right):
    rows, width = left.shape
    block = pl.BlockSpec((rows // 2, width), lambda i: (i, 0))
    return pl.pallas_call(
        add_kernel,
        grid=(2,),
        in_specs=[block, block],
        out_specs=block,
        out_shape=jax.ShapeDtypeStruct(left.shape, jnp.bfloat16),
        compiler_params=pltpu.CompilerParams(vmem_limit_bytes=VMEM),
        cost_estimate=pl.CostEstimate(flops=rows * width, bytes_accessed=6 * rows * width, transcendentals=0),
        name="add",
    )(left, right)


def wide(value):
    return value.astype(jnp.float32)


def with_squares(values, squares):
    high = squares.astype(jnp.bfloat16)
    low = (squares - wide(high)).astype(jnp.bfloat16)
    lane = lax.broadcasted_iota(jnp.int32, (squares.shape[0], 128), 1)
    pieces = jnp.where(lane == 0, wide(high), jnp.where(lane == 1, wide(low), 0.0))
    return jnp.concatenate([values.astype(jnp.bfloat16), pieces.astype(jnp.bfloat16)], axis=1)


def finish_kernel(half_ref, base_ref, left_ref, right_ref, gain_ref, down_ref, *rest):
    stream_ref, latent_ref, scaled = rest[-3:]
    width = left_ref.shape[1]
    step = pl.program_id(0)
    block = down_ref.shape[0]

    @pl.when(step == 0)
    def _():
        left = (base_ref[:, :width] + wide(left_ref[...])).astype(jnp.bfloat16)
        right = (base_ref[:, width:] + wide(right_ref[...])).astype(jnp.bfloat16)
        stream = jnp.concatenate([left, right], axis=1)
        stream_ref[...] = stream
        stream = wide(stream)
        scaled[...] = (stream * gain_ref[...]).astype(jnp.bfloat16)
        squares = jnp.sum(stream * stream, axis=1, keepdims=True)
        nothing = jnp.zeros((squares.shape[0], 128), jnp.float32)
        latent_ref[:, QL:] = with_squares(nothing, squares)[:, 128:]

    value = lax.dot_general(
        scaled[...], down_ref[...], (((1,), (1,)), ((), ())), preferred_element_type=jnp.float32
    )
    latent_ref[:, pl.ds(pl.multiple_of(step * block, block), block)] = value.astype(jnp.bfloat16)


def finish(half, base, left, right, gain, down, stream=None):
    tokens, columns = base.shape
    count = tokens // 2
    block = QL // 2
    part = lambda width: pl.BlockSpec((count, width), lambda n, h: (h[0], 0))
    in_specs = [
        part(columns),
        part(columns // 2),
        part(columns // 2),
        pl.BlockSpec((1, columns), lambda n, h: (0, 0)),
        pl.BlockSpec((block, columns), lambda n, h: (n, 0)),
    ]
    args = [half, base, left, right, gain, down]
    aliases = {}
    if stream is not None:
        in_specs.append(pl.BlockSpec(memory_space=pl.ANY))
        aliases = {len(args): 0}
        args.append(stream)
    return pl.pallas_call(
        finish_kernel,
        grid_spec=pltpu.PrefetchScalarGridSpec(
            num_scalar_prefetch=1,
            grid=(QL // block,),
            in_specs=in_specs,
            out_specs=[part(columns), pl.BlockSpec((count, QL + 128), lambda n, h: (0, 0))],
            scratch_shapes=[pltpu.VMEM((count, columns), jnp.bfloat16)],
        ),
        out_shape=[
            jax.ShapeDtypeStruct((tokens, columns), jnp.bfloat16),
            jax.ShapeDtypeStruct((count, QL + 128), jnp.bfloat16),
        ],
        input_output_aliases=aliases,
        compiler_params=pltpu.CompilerParams(vmem_limit_bytes=VMEM),
        cost_estimate=pl.CostEstimate(
            flops=2 * count * columns * QL, bytes_accessed=2 * columns * QL + 8 * count * columns, transcendentals=0
        ),
        name="finish",
    )(*args)


def fold_kernel(odd_ref, mine_ref, theirs_ref, send_ref, keep_ref):
    rows = send_ref.shape[0]

    def both(which):
        spot = pl.ds(pl.multiple_of(which * rows, rows), rows)
        value = wide(mine_ref[spot, :]) + wide(theirs_ref[spot, :])
        return value[:, :QL], value[:, QL : QL + 1] + value[:, QL + 1 : QL + 2]

    send_ref[...] = with_squares(*both(1 - odd_ref[0]))
    values, squares = both(odd_ref[0])
    keep_ref[:, :QL] = values
    keep_ref[:, QL:] = jnp.broadcast_to(squares, (rows, 128))


def fold(odd, mine, theirs):
    rows, lanes = mine.shape[0] // 2, mine.shape[1]
    whole = pl.BlockSpec(memory_space=pltpu.VMEM)
    return pl.pallas_call(
        fold_kernel,
        in_specs=[pl.BlockSpec(memory_space=pltpu.SMEM), whole, whole],
        out_specs=[whole, whole],
        out_shape=[
            jax.ShapeDtypeStruct((rows, lanes), jnp.bfloat16),
            jax.ShapeDtypeStruct((rows, lanes), jnp.float32),
        ],
        compiler_params=pltpu.CompilerParams(vmem_limit_bytes=VMEM),
        cost_estimate=pl.CostEstimate(flops=8 * rows * lanes, bytes_accessed=14 * rows * lanes, transcendentals=0),
        name="fold",
    )(odd, mine, theirs)


def compress_kernel(mine_ref, theirs_ref, gain_ref, out_ref):
    value = mine_ref[...]
    more = wide(theirs_ref[...])
    squares = value[:, QL : QL + 1] + more[:, QL : QL + 1] + more[:, QL + 1 : QL + 2]
    latent = (value[:, :QL] + more[:, :QL]) * lax.rsqrt(squares / D + EPSILON)
    scale = lax.rsqrt(jnp.sum(latent * latent, axis=1, keepdims=True) / QL + EPSILON)
    out_ref[...] = with_squares(latent * scale * gain_ref[...], squares)


def compress(mine, theirs, gain):
    whole = pl.BlockSpec(memory_space=pltpu.VMEM)
    rows, lanes = theirs.shape
    return pl.pallas_call(
        compress_kernel,
        in_specs=[whole, whole, whole],
        out_specs=whole,
        out_shape=jax.ShapeDtypeStruct(theirs.shape, jnp.bfloat16),
        compiler_params=pltpu.CompilerParams(vmem_limit_bytes=VMEM),
        cost_estimate=pl.CostEstimate(flops=8 * rows * lanes, bytes_accessed=8 * rows * lanes, transcendentals=rows),
        name="compress",
    )(mine, theirs, gain)


def lift_kernel(half_ref, x_ref, weight_ref, stream_ref, gain_ref, *rest):
    queries_ref, normed_ref = rest[-2:]

    @pl.when(pl.program_id(0) == 0)
    def _():
        squares = wide(x_ref[:, QL : QL + 1]) + wide(x_ref[:, QL + 1 : QL + 2])
        scale = lax.rsqrt(squares / D + EPSILON)
        normed_ref[...] = (wide(stream_ref[...]) * scale * gain_ref[...]).astype(jnp.bfloat16)

    value = jnp.dot(x_ref[:, :QL], weight_ref[...], preferred_element_type=jnp.float32)
    queries_ref[...] = value.astype(jnp.bfloat16)


def lift(half, x, weights, stream, gain, before=()):
    count, lanes = x.shape
    depth, columns = weights.shape
    tokens, width = stream.shape
    block = columns // 2
    row = pl.BlockSpec((count, width), lambda n, h: (h[0], 0))
    return pl.pallas_call(
        lift_kernel,
        grid_spec=pltpu.PrefetchScalarGridSpec(
            num_scalar_prefetch=1,
            grid=(columns // block,),
            in_specs=[
                pl.BlockSpec((count, lanes), lambda n, h: (0, 0)),
                pl.BlockSpec((depth, block), lambda n, h: (0, n)),
                row,
                pl.BlockSpec((1, width), lambda n, h: (0, 0)),
            ]
            + [pl.BlockSpec(memory_space=pl.ANY)] * len(before),
            out_specs=[pl.BlockSpec((count, block), lambda n, h: (h[0], n)), row],
        ),
        out_shape=[
            jax.ShapeDtypeStruct((tokens, columns), jnp.bfloat16),
            jax.ShapeDtypeStruct((tokens, width), jnp.bfloat16),
        ],
        input_output_aliases={5: 0, 6: 1} if before else {},
        compiler_params=pltpu.CompilerParams(vmem_limit_bytes=VMEM),
        cost_estimate=pl.CostEstimate(
            flops=2 * count * depth * columns,
            bytes_accessed=2 * depth * columns + 2 * count * columns,
            transcendentals=0,
        ),
        name="lift",
    )(half, x, weights, stream, gain, *before)


def shards(expert_out, expert_ids, gate_levels, residual, attn_gain, wq_a, latent_gain, wq_b):
    half = lax.axis_index("dp")
    place = lax.axis_index("expert")
    quarter = jnp.asarray(QUARTERS)[half, lax.axis_index("tensor")]
    upper, odd = quarter // 2, quarter % 2
    tokens = expert_ids.shape[0]
    columns = residual.shape[1]
    width = columns // GROUPS

    part = wq_b.shape[0] // 2

    def spread_out(value):
        return lax.all_gather(value, ("dp", "expert"), axis=0, tiled=True)

    down = spread_out(lax.dynamic_slice_in_dim(wq_a.T, half * part, part, 0))
    up_part = lax.dynamic_slice_in_dim(wq_b, half * part, part, 0)
    gain = latent_gain.reshape(RING, 2, part).transpose(1, 0, 2).reshape(1, QL)

    owners = jnp.asarray(owner_table())[half, place]
    spots = jnp.asarray(spot_table())[half, place]
    holders = jnp.asarray(holder_table())[half, place]
    experts = (holders[:, None] * HOLD + jnp.arange(HOLD, dtype=jnp.int32)[None, :]).reshape(-1)
    experts = jnp.concatenate([experts, jnp.full((64 - experts.shape[0],), -1, jnp.int32)])
    experts = jnp.broadcast_to(experts.astype(jnp.float32)[:, None], (64, tokens))

    spot = jnp.arange(RING * RING, dtype=jnp.int32)
    slots = expert_out.transpose(0, 2, 1, 3).reshape(SLOTS, RING, columns)
    relayed = []
    for g in range(GROUPS):
        source = (spot % RING) * RING + jnp.repeat(owners[g], RING)
        move = (source[:, None] == spot[None, :]).astype(jnp.bfloat16)
        relayed.append(relay(slots, move, g))
    packed = [jnp.concatenate([expert_ids.T, gate_levels.T], axis=0)]
    for i, kind in enumerate(ORDERS[0]):
        received = lax.ppermute(packed[-1], "expert", [(e, partner(kind, e)) for e in range(RING)])
        if i in (1, 2):
            received, _ = lax.optimization_barrier((received, relayed[i - 1][0]))
        packed.append(jnp.concatenate([packed[-1], received], axis=0))
    first = []
    for g in range(GROUPS):
        left, right, _ = lax.optimization_barrier((relayed[g][0], relayed[g][1], packed[2 * g + 2]))
        first.append([swap(left, g, 0), swap(right, g, 0)])

    position = jnp.arange(tokens, dtype=jnp.int32)
    later = (position[:, None] < position[None, :]).astype(jnp.bfloat16)
    routes = route(packed[-1].reshape(RING, 16, tokens), experts, later, tokens)
    slot = np.arange(SLOTS)
    turn = np.broadcast_to(STEP * np.tile(slot % CAP, 2)[None, :], (8, 2 * SLOTS))
    turn = jnp.asarray(turn.astype(np.float32))
    lanes = np.arange(64)[:, None]
    spread = []
    for g in range(GROUPS):
        expert = (slot // CAP)[None, :]
        hit = np.concatenate([lanes == expert, lanes == expert + HOLD * (g + 1)], axis=1)
        spread.append(jnp.asarray(np.concatenate([hit, STEP * hit], axis=0).astype(np.float32)).astype(jnp.bfloat16))

    def summed(g, start, more=()):
        received = first[g][start // 4]
        return combine(spots[g], routes, spread[g], turn, relayed[g][2], received, start, 2, tokens, more)

    groups = range(GROUPS)
    passed = [[summed(g, 2 * i) for g in groups] for i in range(2)]
    second_a = [swap(passed[0][g], g, 1) for g in groups]
    second_b = [swap(passed[1][g], g, 1) for g in groups]
    kept_a = [summed(g, 4, (second_a[g],)) for g in groups]
    third_a = [swap(kept_a[g][0], g, 2) for g in groups]
    third_b = [swap(kept_a[g][1], g, 2) for g in groups]
    kept_b = [summed(g, 6, (second_b[g],)) for g in groups]
    last = [add(kept_b[g][0], third_a[g]) for g in groups]
    fourth = [swap(last[g], g, 3) for g in groups]
    up_part, *_ = lax.optimization_barrier((up_part, *last))
    up = spread_out(up_part)
    base = jnp.concatenate(
        [
            wide(residual[:, g * width : (g + 1) * width])
            + wide(kept_b[g][1])
            + wide(third_b[g])
            for g in range(GROUPS)
        ],
        axis=1,
    )

    here = upper.reshape(1)
    there = 1 - here
    wide_gain = attn_gain.reshape(1, columns)
    stream, latent_there = finish(there, base, *fourth, wide_gain, down)
    latent_theirs = turn_to(latent_there, 0)
    stream, latent_here = finish(here, base, *fourth, wide_gain, down, stream)
    latent_send, latent_keep = fold(odd.reshape(1), latent_here, latent_theirs)
    normed_mine = compress(latent_keep, turn_to(latent_send, 1), gain)
    normed_theirs = turn_to(normed_mine, 1)
    half_here = jnp.where(
        odd == 0,
        jnp.concatenate([normed_mine, normed_theirs], axis=0),
        jnp.concatenate([normed_theirs, normed_mine], axis=0),
    )
    half_there = turn_to(half_here, 0)
    queries, normed = lift(here, half_here, up, stream, wide_gain)
    queries, normed = lift(there, half_there, up, stream, wide_gain, (queries, normed))
    return (stream, normed, queries)


def solution(mesh):
    return jax.shard_map(
        shards,
        mesh=mesh,
        in_specs=(
            P(("dp", "expert"), None, None, "tensor"),
            P(("dp", "expert"), None),
            P(("dp", "expert"), None),
            P(("dp", "expert"), "tensor"),
            P("tensor"),
            P("tensor", "expert"),
            P(),
            P("expert", "tensor"),
        ),
        out_specs=(
            P(("dp", "expert"), "tensor"),
            P(("dp", "expert"), "tensor"),
            P(("dp", "expert"), "tensor"),
        ),
        check_vma=False,
    )
```

```python
import functools

import jax
import jax.numpy as jnp
import numpy as np
from jax import lax
from jax.experimental import pallas as pl
from jax.experimental.pallas import tpu as pltpu
from jax.sharding import PartitionSpec as P

D = 7168
QL = 1536
CAP = 20
HOLD = 16
SLOTS = HOLD * CAP
SIDE = 4
RING = 16
ROUTE_SCALE = 2.5
EPSILON = 1e-06
STEP = 4.0
VMEM = 60 << 20

ORDERS = ("PQpq", "QpqP", "pqPQ", "qPQp")
GROUPS = 2
EVEN = (1, 0, 3, 2)
ODD = (3, 2, 1, 0)


def partner(kind, place):
    slow, fast = divmod(place, SIDE)
    if kind == "P":
        slow = EVEN[slow]
    elif kind == "Q":
        slow = ODD[slow]
    elif kind == "p":
        fast = EVEN[fast]
    else:
        fast = ODD[fast]
    return slow * SIDE + fast


def order_of(group, half):
    return ORDERS[2 * group + half]


def keep(order, step, place):
    if step == 4:
        return [place]
    return keep(order, step + 1, partner(order[step], place)) + keep(order, step + 1, place)


def owner_table():
    return np.array(
        [[[keep(order_of(g, h), 0, e) for g in range(GROUPS)] for e in range(RING)] for h in range(2)],
        np.int32,
    )


def holder_table():
    return np.array(
        [
            [[e] + [partner(order_of(g, h)[0], e) for g in range(GROUPS)] for e in range(RING)]
            for h in range(2)
        ],
        np.int32,
    )


def gathered(place, steps):
    if not steps:
        return [place]
    return gathered(place, steps[:-1]) + gathered(partner(steps[-1], place), steps[:-1])


def spot_table():
    places = [gathered(e, ORDERS[0]) for e in range(RING)]
    owners = owner_table()
    return np.array(
        [
            [[[places[e].index(o) for o in owners[h, e, g]] for g in range(GROUPS)] for e in range(RING)]
            for h in range(2)
        ],
        np.int32,
    )


def swap(value, group, step):
    pairs = [
        (half * RING + e, half * RING + partner(order_of(group, half)[step], e))
        for half in range(2)
        for e in range(RING)
    ]
    return lax.ppermute(value, ("dp", "expert"), pairs)


RING_STEPS = ((EVEN, ODD), (ODD, EVEN))
QUARTERS = np.array([[0, 2, 3, 1], [0, 1, 3, 2]], np.int32)


def turn_to(value, step):
    pairs = [(h * 4 + y, h * 4 + RING_STEPS[h][step][y]) for h in range(2) for y in range(4)]
    return lax.ppermute(value, ("dp", "tensor"), pairs)


def relay_kernel(move_ref, x_ref, first_ref, second_ref, keep_ref):
    for b in range(x_ref.shape[0] // RING):
        rows = slice(b * RING, (b + 1) * RING)
        block = x_ref[rows].reshape(RING * RING, x_ref.shape[2])
        moved = jnp.dot(move_ref[...], block, preferred_element_type=jnp.float32).astype(jnp.bfloat16)
        moved = moved.reshape(RING, RING, x_ref.shape[2])
        first_ref[:, rows] = moved[0:4]
        second_ref[:, rows] = moved[4:8]
        keep_ref[:, rows] = moved[8:16]


def relay(slots, move, group):
    width = slots.shape[2] // GROUPS
    rows = SLOTS // 2
    out = lambda n: pl.BlockSpec((n, rows, width), lambda i: (0, i, 0))
    return pl.pallas_call(
        relay_kernel,
        grid=(SLOTS // rows,),
        in_specs=[
            pl.BlockSpec((RING * RING, RING * RING), lambda i: (0, 0)),
            pl.BlockSpec((rows, RING, width), lambda i: (i, 0, group)),
        ],
        out_specs=[out(4), out(4), out(8)],
        out_shape=[jax.ShapeDtypeStruct((n, SLOTS, width), jnp.bfloat16) for n in (4, 4, 8)],
        compiler_params=pltpu.CompilerParams(vmem_limit_bytes=VMEM),
        cost_estimate=pl.CostEstimate(
            flops=2 * RING * SLOTS * RING * RING * width,
            bytes_accessed=4 * RING * SLOTS * width,
            transcendentals=0,
        ),
        name="relay",
    )(move, slots)


def route_kernel(packed_ref, expert_ref, later_ref, out_ref):
    tokens = packed_ref.shape[2]
    rows = expert_ref.shape[0]
    experts = expert_ref[...]
    for i in range(packed_ref.shape[0]):
        table = packed_ref[i].astype(jnp.float32)
        levels = table[8:16]
        weight = ROUTE_SCALE * levels / jnp.sum(levels, axis=0, keepdims=True)
        named = jnp.zeros((rows, tokens), jnp.float32)
        weighed = jnp.zeros((rows, tokens), jnp.float32)
        for k in range(8):
            hit = experts == table[k : k + 1]
            named = jnp.where(hit, 1.0, named)
            weighed = jnp.where(hit, weight[k : k + 1], weighed)
        rank = jnp.dot(named.astype(jnp.bfloat16), later_ref[...], preferred_element_type=jnp.float32)
        out_ref[i] = jnp.concatenate([weighed, rank], axis=0).T.astype(jnp.bfloat16)


def route(packed, experts, later, tokens):
    rows = experts.shape[0]
    count = 8
    return pl.pallas_call(
        route_kernel,
        grid=(RING // count,),
        in_specs=[
            pl.BlockSpec((count, 16, tokens), lambda i: (i, 0, 0)),
            pl.BlockSpec((rows, tokens), lambda i: (0, 0)),
            pl.BlockSpec((tokens, tokens), lambda i: (0, 0)),
        ],
        out_specs=pl.BlockSpec((count, tokens, 2 * rows), lambda i: (i, 0, 0)),
        out_shape=jax.ShapeDtypeStruct((RING, tokens, 2 * rows), jnp.bfloat16),
        compiler_params=pltpu.CompilerParams(vmem_limit_bytes=VMEM),
        cost_estimate=pl.CostEstimate(
            flops=RING * 2 * tokens * tokens * 256, bytes_accessed=RING * tokens * 256, transcendentals=0
        ),
        name="route",
    )(packed, experts, later)


def combine_kernel(spot_ref, route_ref, spread_ref, turn_ref, mine_ref, theirs_ref, *rest, outs):
    rows = rest[-1]
    rows[0:SLOTS] = mine_ref[0]
    rows[SLOTS : 2 * SLOTS] = theirs_ref[0]
    level = jnp.dot(route_ref[0], spread_ref[...], preferred_element_type=jnp.float32) - turn_ref[0:1, :]
    matrix = jnp.where(jnp.abs(level - 1.25) < 1.5, level, 0.0).astype(jnp.bfloat16)
    value = jnp.dot(matrix, rows[...], preferred_element_type=jnp.float32)
    if len(rest) > 1 + outs:
        value += wide(rest[0][0])
    value = value.astype(jnp.bfloat16)
    if outs == 1:
        rest[-2][0] = value
    else:
        for i in range(outs):

            @pl.when(pl.program_id(0) == i)
            def _():
                rest[i - 1 - outs][...] = value


def combine(spots, routes, spread, turn, mine, theirs, first, count, tokens, more=()):
    width = mine.shape[2]
    lanes = routes.shape[2]
    outs = count if more else 1
    if more:
        out_specs = [pl.BlockSpec((tokens, width), lambda i, o: (0, 0))] * count
        out_shape = [jax.ShapeDtypeStruct((tokens, width), jnp.bfloat16)] * count
    else:
        out_specs = pl.BlockSpec((1, tokens, width), lambda i, o: (i, 0, 0))
        out_shape = jax.ShapeDtypeStruct((count, tokens, width), jnp.bfloat16)
    return pl.pallas_call(
        functools.partial(combine_kernel, outs=outs),
        grid_spec=pltpu.PrefetchScalarGridSpec(
            num_scalar_prefetch=1,
            grid=(count,),
            in_specs=[
                pl.BlockSpec((1, tokens, lanes), lambda i, o: (o[8 + first + i], 0, 0)),
                pl.BlockSpec((lanes, 2 * SLOTS), lambda i, o: (0, 0)),
                pl.BlockSpec((8, 2 * SLOTS), lambda i, o: (0, 0)),
                pl.BlockSpec((1, SLOTS, width), lambda i, o: (first + i, 0, 0)),
                pl.BlockSpec((1, SLOTS, width), lambda i, o: (first % 4 + i, 0, 0)),
            ]
            + [pl.BlockSpec((1, tokens, width), lambda i, o: (i, 0, 0))] * len(more),
            out_specs=out_specs,
            scratch_shapes=[pltpu.VMEM((2 * SLOTS, width), jnp.bfloat16)],
        ),
        out_shape=out_shape,
        compiler_params=pltpu.CompilerParams(vmem_limit_bytes=VMEM),
        cost_estimate=pl.CostEstimate(
            flops=count * 2 * tokens * 2 * SLOTS * (width + 256),
            bytes_accessed=count * (tokens * width + 2 * SLOTS * width + tokens * lanes) * 2,
            transcendentals=0,
        ),
        name="combine",
    )(spots, routes, spread, turn, mine, theirs, *more)


def add_kernel(left_ref, right_ref, out_ref):
    out_ref[...] = (wide(left_ref[...]) + wide(right_ref[...])).astype(jnp.bfloat16)


def add(left, right):
    rows, width = left.shape
    block = pl.BlockSpec((rows // 2, width), lambda i: (i, 0))
    return pl.pallas_call(
        add_kernel,
        grid=(2,),
        in_specs=[block, block],
        out_specs=block,
        out_shape=jax.ShapeDtypeStruct(left.shape, jnp.bfloat16),
        compiler_params=pltpu.CompilerParams(vmem_limit_bytes=VMEM),
        cost_estimate=pl.CostEstimate(flops=rows * width, bytes_accessed=6 * rows * width, transcendentals=0),
        name="add",
    )(left, right)


def wide(value):
    return value.astype(jnp.float32)


def with_squares(values, squares):
    high = squares.astype(jnp.bfloat16)
    low = (squares - wide(high)).astype(jnp.bfloat16)
    lane = lax.broadcasted_iota(jnp.int32, (squares.shape[0], 128), 1)
    pieces = jnp.where(lane == 0, wide(high), jnp.where(lane == 1, wide(low), 0.0))
    return jnp.concatenate([values.astype(jnp.bfloat16), pieces.astype(jnp.bfloat16)], axis=1)


def finish_kernel(place_ref, base_ref, left_ref, right_ref, gain_ref, down_ref, stream_ref, *rest):
    parts, scaled, sums = rest[:4], rest[4], rest[5]
    width = left_ref.shape[1]
    rows = parts[0].shape[0]
    step = pl.program_id(0)
    block = down_ref.shape[0]

    @pl.when(step == 0)
    def _():
        for i in range(4):
            here = slice(i * rows, (i + 1) * rows)
            left = (base_ref[here, :width] + wide(left_ref[here])).astype(jnp.bfloat16)
            right = (base_ref[here, width:] + wide(right_ref[here])).astype(jnp.bfloat16)
            stream = jnp.concatenate([left, right], axis=1)
            stream_ref[here] = stream
            stream = wide(stream)
            squares = jnp.sum(stream * stream, axis=1, keepdims=True)
            nothing = jnp.zeros((rows, 128), jnp.float32)
            rank = 2 * jnp.where(place_ref[0] == i // 2, 0, 1) + jnp.where(place_ref[1] == i % 2, 0, 1)
            spot = pl.ds(pl.multiple_of(rank * rows, rows), rows)
            scaled[spot, :] = (stream * gain_ref[...]).astype(jnp.bfloat16)
            sums[spot, :] = with_squares(nothing, squares)[:, 128:]
        for i in range(4):
            parts[i][:, QL:] = sums[i * rows : (i + 1) * rows]

    value = lax.dot_general(
        scaled[...], down_ref[...], (((1,), (1,)), ((), ())), preferred_element_type=jnp.float32
    ).astype(jnp.bfloat16)
    lanes = pl.ds(pl.multiple_of(step * block, block), block)
    for i in range(4):
        parts[i][:, lanes] = value[i * rows : (i + 1) * rows]


def finish(place, base, left, right, gain, down):
    tokens, columns = base.shape
    rows = tokens // 4
    block = QL // 3
    whole = lambda *shape: pl.BlockSpec(shape, lambda n, p: (0, 0))
    return pl.pallas_call(
        finish_kernel,
        grid_spec=pltpu.PrefetchScalarGridSpec(
            num_scalar_prefetch=1,
            grid=(QL // block,),
            in_specs=[
                whole(tokens, columns),
                whole(tokens, columns // 2),
                whole(tokens, columns // 2),
                whole(1, columns),
                pl.BlockSpec((block, columns), lambda n, p: (n, 0)),
            ],
            out_specs=[whole(tokens, columns)] + [whole(rows, QL + 128)] * 4,
            scratch_shapes=[
                pltpu.VMEM((tokens, columns), jnp.bfloat16),
                pltpu.VMEM((tokens, 128), jnp.bfloat16),
            ],
        ),
        out_shape=[jax.ShapeDtypeStruct((tokens, columns), jnp.bfloat16)]
        + [jax.ShapeDtypeStruct((rows, QL + 128), jnp.bfloat16)] * 4,
        compiler_params=pltpu.CompilerParams(vmem_limit_bytes=VMEM),
        cost_estimate=pl.CostEstimate(
            flops=2 * tokens * columns * QL,
            bytes_accessed=2 * columns * QL + 10 * tokens * columns,
            transcendentals=0,
        ),
        name="finish",
    )(place, base, left, right, gain, down)


def compress_kernel(*refs):
    gain_ref, out_ref = refs[-2:]
    latent = sum(wide(ref[:, :QL]) for ref in refs[:-2])
    squares = sum(wide(ref[:, QL : QL + 1]) + wide(ref[:, QL + 1 : QL + 2]) for ref in refs[:-2])
    latent = latent * lax.rsqrt(squares / D + EPSILON)
    scale = lax.rsqrt(jnp.sum(latent * latent, axis=1, keepdims=True) / QL + EPSILON)
    out_ref[...] = with_squares(latent * scale * gain_ref[...], squares)


def compress(parts, gain):
    whole = pl.BlockSpec(memory_space=pltpu.VMEM)
    rows, lanes = parts[0].shape
    return pl.pallas_call(
        compress_kernel,
        in_specs=[whole] * (len(parts) + 1),
        out_specs=whole,
        out_shape=jax.ShapeDtypeStruct((rows, lanes), jnp.bfloat16),
        compiler_params=pltpu.CompilerParams(vmem_limit_bytes=VMEM),
        cost_estimate=pl.CostEstimate(flops=8 * rows * lanes, bytes_accessed=10 * rows * lanes, transcendentals=rows),
        name="compress",
    )(*parts, gain)


def lift_kernel(half_ref, x_ref, weight_ref, stream_ref, gain_ref, *rest):
    queries_ref, normed_ref = rest[-2:]

    @pl.when(pl.program_id(0) == 0)
    def _():
        squares = wide(x_ref[:, QL : QL + 1]) + wide(x_ref[:, QL + 1 : QL + 2])
        scale = lax.rsqrt(squares / D + EPSILON)
        normed_ref[...] = (wide(stream_ref[...]) * scale * gain_ref[...]).astype(jnp.bfloat16)

    value = jnp.dot(x_ref[:, :QL], weight_ref[...], preferred_element_type=jnp.float32)
    queries_ref[...] = value.astype(jnp.bfloat16)


def lift(half, x, weights, stream, gain, before=()):
    count, lanes = x.shape
    depth, columns = weights.shape
    tokens, width = stream.shape
    block = columns // 2
    row = pl.BlockSpec((count, width), lambda n, h: (h[0], 0))
    return pl.pallas_call(
        lift_kernel,
        grid_spec=pltpu.PrefetchScalarGridSpec(
            num_scalar_prefetch=1,
            grid=(columns // block,),
            in_specs=[
                pl.BlockSpec((count, lanes), lambda n, h: (0, 0)),
                pl.BlockSpec((depth, block), lambda n, h: (0, n)),
                row,
                pl.BlockSpec((1, width), lambda n, h: (0, 0)),
            ]
            + [pl.BlockSpec(memory_space=pl.ANY)] * len(before),
            out_specs=[pl.BlockSpec((count, block), lambda n, h: (h[0], n)), row],
        ),
        out_shape=[
            jax.ShapeDtypeStruct((tokens, columns), jnp.bfloat16),
            jax.ShapeDtypeStruct((tokens, width), jnp.bfloat16),
        ],
        input_output_aliases={5: 0, 6: 1} if before else {},
        compiler_params=pltpu.CompilerParams(vmem_limit_bytes=VMEM),
        cost_estimate=pl.CostEstimate(
            flops=2 * count * depth * columns,
            bytes_accessed=2 * depth * columns + 2 * count * columns,
            transcendentals=0,
        ),
        name="lift",
    )(half, x, weights, stream, gain, *before)


def shards(expert_out, expert_ids, gate_levels, residual, attn_gain, wq_a, latent_gain, wq_b):
    half = lax.axis_index("dp")
    place = lax.axis_index("expert")
    quarter = jnp.asarray(QUARTERS)[half, lax.axis_index("tensor")]
    upper, odd = quarter // 2, quarter % 2
    tokens = expert_ids.shape[0]
    columns = residual.shape[1]
    width = columns // GROUPS

    part = wq_b.shape[0] // 2

    def spread_out(value):
        return lax.all_gather(value, ("dp", "expert"), axis=0, tiled=True)

    down = spread_out(lax.dynamic_slice_in_dim(wq_a.T, half * part, part, 0))
    up_part = lax.dynamic_slice_in_dim(wq_b, half * part, part, 0)
    gain = latent_gain.reshape(RING, 2, part).transpose(1, 0, 2).reshape(1, QL)

    owners = jnp.asarray(owner_table())[half, place]
    spots = jnp.asarray(spot_table())[half, place]
    holders = jnp.asarray(holder_table())[half, place]
    experts = (holders[:, None] * HOLD + jnp.arange(HOLD, dtype=jnp.int32)[None, :]).reshape(-1)
    experts = jnp.concatenate([experts, jnp.full((64 - experts.shape[0],), -1, jnp.int32)])
    experts = jnp.broadcast_to(experts.astype(jnp.float32)[:, None], (64, tokens))

    packed = [jnp.concatenate([expert_ids.T, gate_levels.T], axis=0)]

    def double(kind, beside=()):
        received = lax.ppermute(packed[-1], "expert", [(e, partner(kind, e)) for e in range(RING)])
        received, *_ = lax.optimization_barrier((received, *beside))
        packed.append(jnp.concatenate([packed[-1], received], axis=0))

    double(ORDERS[0][0])
    double(ORDERS[0][1])
    spot = jnp.arange(RING * RING, dtype=jnp.int32)
    slots = expert_out.transpose(0, 2, 1, 3).reshape(SLOTS, RING, columns)
    relayed, first = [], []
    for g in range(GROUPS):
        source = (spot % RING) * RING + jnp.repeat(owners[g], RING)
        move = (source[:, None] == spot[None, :]).astype(jnp.bfloat16)
        move, _ = lax.optimization_barrier((move, packed[2 + g]))
        relayed.append(relay(slots, move, g))
        double(ORDERS[0][2 + g], relayed[g][:1])
        left, right, _ = lax.optimization_barrier((relayed[g][0], relayed[g][1], packed[2 * g + 2]))
        first.append([swap(left, g, 0), swap(right, g, 0)])

    position = jnp.arange(tokens, dtype=jnp.int32)
    later = (position[:, None] < position[None, :]).astype(jnp.bfloat16)
    routes = route(packed[-1].reshape(RING, 16, tokens), experts, later, tokens)
    slot = np.arange(SLOTS)
    turn = np.broadcast_to(STEP * np.tile(slot % CAP, 2)[None, :], (8, 2 * SLOTS))
    turn = jnp.asarray(turn.astype(np.float32))
    lanes = np.arange(64)[:, None]
    spread = []
    for g in range(GROUPS):
        expert = (slot // CAP)[None, :]
        hit = np.concatenate([lanes == expert, lanes == expert + HOLD * (g + 1)], axis=1)
        spread.append(jnp.asarray(np.concatenate([hit, STEP * hit], axis=0).astype(np.float32)).astype(jnp.bfloat16))

    def summed(g, start, more=()):
        received = first[g][start // 4]
        return combine(spots[g], routes, spread[g], turn, relayed[g][2], received, start, 2, tokens, more)

    groups = range(GROUPS)
    passed = [[summed(g, 2 * i) for g in groups] for i in range(2)]
    second_a = [swap(passed[0][g], g, 1) for g in groups]
    second_b = [swap(passed[1][g], g, 1) for g in groups]
    kept_a = [summed(g, 4, (second_a[g],)) for g in groups]
    third_a = [swap(kept_a[g][0], g, 2) for g in groups]
    third_b = [swap(kept_a[g][1], g, 2) for g in groups]
    kept_b = [summed(g, 6, (second_b[g],)) for g in groups]
    last = []
    for g in groups:
        arrived, _ = lax.optimization_barrier((third_a[g], third_b[g]))
        last.append(add(kept_b[g][0], arrived))
    fourth = [swap(last[g], g, 3) for g in groups]
    up_part, *_ = lax.optimization_barrier((up_part, *last))
    up = spread_out(up_part)
    base = jnp.concatenate(
        [
            wide(residual[:, g * width : (g + 1) * width])
            + wide(kept_b[g][1])
            + wide(third_b[g])
            for g in range(GROUPS)
        ],
        axis=1,
    )

    here = upper.reshape(1)
    there = 1 - here
    wide_gain = attn_gain.reshape(1, columns)
    count = lax.axis_size("tensor")
    across = [(y, (y + 2) % count) for y in range(count)]
    place_here = jnp.stack([upper, odd])
    stream, own, beside, near, far = finish(place_here, base, *fourth, wide_gain, down)
    far = lax.ppermute(far, "tensor", across)
    near = turn_to(near, 0)
    normed_mine = compress((own, turn_to(beside, 1), near, far), gain)
    normed_theirs = turn_to(normed_mine, 1)
    half_here = jnp.where(
        odd == 0,
        jnp.concatenate([normed_mine, normed_theirs], axis=0),
        jnp.concatenate([normed_theirs, normed_mine], axis=0),
    )
    half_there = turn_to(half_here, 0)
    queries, normed = lift(here, half_here, up, stream, wide_gain)
    queries, normed = lift(there, half_there, up, stream, wide_gain, (queries, normed))
    return (stream, normed, queries)


def solution(mesh):
    return jax.shard_map(
        shards,
        mesh=mesh,
        in_specs=(
            P(("dp", "expert"), None, None, "tensor"),
            P(("dp", "expert"), None),
            P(("dp", "expert"), None),
            P(("dp", "expert"), "tensor"),
            P("tensor"),
            P("tensor", "expert"),
            P(),
            P("expert", "tensor"),
        ),
        out_specs=(
            P(("dp", "expert"), "tensor"),
            P(("dp", "expert"), "tensor"),
            P(("dp", "expert"), "tensor"),
        ),
        check_vma=False,
    )
```

```python
import functools

import jax
import jax.numpy as jnp
import numpy as np
from jax import lax
from jax.experimental import pallas as pl
from jax.experimental.pallas import tpu as pltpu
from jax.sharding import PartitionSpec as P

D = 7168
QL = 1536
CAP = 20
HOLD = 16
SLOTS = HOLD * CAP
SIDE = 4
RING = 16
ROUTE_SCALE = 2.5
EPSILON = 1e-06
STEP = 4.0
VMEM = 60 << 20

ORDERS = ("PQpq", "QpqP", "pqPQ", "qPQp")
GROUPS = 2
EVEN = (1, 0, 3, 2)
ODD = (3, 2, 1, 0)


def partner(kind, place):
    slow, fast = divmod(place, SIDE)
    if kind == "P":
        slow = EVEN[slow]
    elif kind == "Q":
        slow = ODD[slow]
    elif kind == "p":
        fast = EVEN[fast]
    else:
        fast = ODD[fast]
    return slow * SIDE + fast


def order_of(group, half):
    return ORDERS[2 * group + half]


def keep(order, step, place):
    if step == 4:
        return [place]
    return keep(order, step + 1, partner(order[step], place)) + keep(order, step + 1, place)


def owner_table():
    return np.array(
        [[[keep(order_of(g, h), 0, e) for g in range(GROUPS)] for e in range(RING)] for h in range(2)],
        np.int32,
    )


def holder_table():
    return np.array(
        [
            [[e] + [partner(order_of(g, h)[0], e) for g in range(GROUPS)] for e in range(RING)]
            for h in range(2)
        ],
        np.int32,
    )


def gathered(place, steps):
    if not steps:
        return [place]
    return gathered(place, steps[:-1]) + gathered(partner(steps[-1], place), steps[:-1])


def spot_table():
    places = [gathered(e, ORDERS[0]) for e in range(RING)]
    owners = owner_table()
    return np.array(
        [
            [[[places[e].index(o) for o in owners[h, e, g]] for g in range(GROUPS)] for e in range(RING)]
            for h in range(2)
        ],
        np.int32,
    )


def swap(value, group, step):
    pairs = [
        (half * RING + e, half * RING + partner(order_of(group, half)[step], e))
        for half in range(2)
        for e in range(RING)
    ]
    return lax.ppermute(value, ("dp", "expert"), pairs)


RING_STEPS = ((EVEN, ODD), (ODD, EVEN))
QUARTERS = np.array([[0, 2, 3, 1], [0, 1, 3, 2]], np.int32)


def turn_to(value, step):
    pairs = [(h * 4 + y, h * 4 + RING_STEPS[h][step][y]) for h in range(2) for y in range(4)]
    return lax.ppermute(value, ("dp", "tensor"), pairs)


def relay_kernel(move_ref, x_ref, first_ref, second_ref, keep_ref):
    for b in range(x_ref.shape[0] // RING):
        rows = slice(b * RING, (b + 1) * RING)
        block = x_ref[rows].reshape(RING * RING, x_ref.shape[2])
        moved = jnp.dot(move_ref[...], block, preferred_element_type=jnp.float32).astype(jnp.bfloat16)
        moved = moved.reshape(RING, RING, x_ref.shape[2])
        first_ref[:, rows] = moved[0:4]
        second_ref[:, rows] = moved[4:8]
        keep_ref[:, rows] = moved[8:16]


def relay(slots, move, group):
    width = slots.shape[2] // GROUPS
    rows = SLOTS // 2
    out = lambda n: pl.BlockSpec((n, rows, width), lambda i: (0, i, 0))
    return pl.pallas_call(
        relay_kernel,
        grid=(SLOTS // rows,),
        in_specs=[
            pl.BlockSpec((RING * RING, RING * RING), lambda i: (0, 0)),
            pl.BlockSpec((rows, RING, width), lambda i: (i, 0, group)),
        ],
        out_specs=[out(4), out(4), out(8)],
        out_shape=[jax.ShapeDtypeStruct((n, SLOTS, width), jnp.bfloat16) for n in (4, 4, 8)],
        compiler_params=pltpu.CompilerParams(vmem_limit_bytes=VMEM),
        cost_estimate=pl.CostEstimate(
            flops=2 * RING * SLOTS * RING * RING * width,
            bytes_accessed=4 * RING * SLOTS * width,
            transcendentals=0,
        ),
        name="relay",
    )(move, slots)


def route_kernel(packed_ref, expert_ref, later_ref, out_ref):
    tokens = packed_ref.shape[2]
    rows = expert_ref.shape[0]
    experts = expert_ref[...]
    for i in range(packed_ref.shape[0]):
        table = packed_ref[i].astype(jnp.float32)
        levels = table[8:16]
        weight = ROUTE_SCALE * levels / jnp.sum(levels, axis=0, keepdims=True)
        named = jnp.zeros((rows, tokens), jnp.float32)
        weighed = jnp.zeros((rows, tokens), jnp.float32)
        for k in range(8):
            hit = experts == table[k : k + 1]
            named = jnp.where(hit, 1.0, named)
            weighed = jnp.where(hit, weight[k : k + 1], weighed)
        rank = jnp.dot(named.astype(jnp.bfloat16), later_ref[...], preferred_element_type=jnp.float32)
        out_ref[i] = jnp.concatenate([weighed, rank], axis=0).T.astype(jnp.bfloat16)


def route(packed, experts, later, tokens):
    rows = experts.shape[0]
    count = 8
    return pl.pallas_call(
        route_kernel,
        grid=(RING // count,),
        in_specs=[
            pl.BlockSpec((count, 16, tokens), lambda i: (i, 0, 0)),
            pl.BlockSpec((rows, tokens), lambda i: (0, 0)),
            pl.BlockSpec((tokens, tokens), lambda i: (0, 0)),
        ],
        out_specs=pl.BlockSpec((count, tokens, 2 * rows), lambda i: (i, 0, 0)),
        out_shape=jax.ShapeDtypeStruct((RING, tokens, 2 * rows), jnp.bfloat16),
        compiler_params=pltpu.CompilerParams(vmem_limit_bytes=VMEM),
        cost_estimate=pl.CostEstimate(
            flops=RING * 2 * tokens * tokens * 256, bytes_accessed=RING * tokens * 256, transcendentals=0
        ),
        name="route",
    )(packed, experts, later)


def combine_kernel(spot_ref, route_ref, spread_ref, turn_ref, mine_ref, theirs_ref, *rest, more, outs):
    added, results, rows = rest[:more], rest[more : more + outs], rest[-1]
    rows[0:SLOTS] = mine_ref[0]
    rows[SLOTS : 2 * SLOTS] = theirs_ref[0]
    level = jnp.dot(route_ref[0], spread_ref[...], preferred_element_type=jnp.float32) - turn_ref[0:1, :]
    matrix = jnp.where(jnp.abs(level - 1.25) < 1.5, level, 0.0).astype(jnp.bfloat16)
    value = jnp.dot(matrix, rows[...], preferred_element_type=jnp.float32)
    if not more:
        results[0][0] = value.astype(jnp.bfloat16)
        return
    value += wide(added[0][0])
    for i in range(outs):

        @pl.when(pl.program_id(0) == i)
        def _():
            total = value
            for one in added[1:2] if i == 0 else added[2:]:
                total = total + wide(one[...])
            results[i][...] = total.astype(results[i].dtype)


def combine(spots, routes, spread, turn, mine, theirs, first, count, tokens, more=(), group=None):
    width = mine.shape[2]
    lanes = routes.shape[2]
    outs = count if more else 1
    if more:
        out_specs = [pl.BlockSpec((tokens, width), lambda i, o: (0, 0))] * count
        kinds = (jnp.bfloat16, jnp.bfloat16 if group is None else jnp.float32)
        out_shape = [jax.ShapeDtypeStruct((tokens, width), kind) for kind in kinds]
    else:
        out_specs = pl.BlockSpec((1, tokens, width), lambda i, o: (i, 0, 0))
        out_shape = jax.ShapeDtypeStruct((count, tokens, width), jnp.bfloat16)
    return pl.pallas_call(
        functools.partial(combine_kernel, more=len(more), outs=outs),
        grid_spec=pltpu.PrefetchScalarGridSpec(
            num_scalar_prefetch=1,
            grid=(count,),
            in_specs=[
                pl.BlockSpec((1, tokens, lanes), lambda i, o: (o[8 + first + i], 0, 0)),
                pl.BlockSpec((lanes, 2 * SLOTS), lambda i, o: (0, 0)),
                pl.BlockSpec((8, 2 * SLOTS), lambda i, o: (0, 0)),
                pl.BlockSpec((1, SLOTS, width), lambda i, o: (first + i, 0, 0)),
                pl.BlockSpec((1, SLOTS, width), lambda i, o: (first % 4 + i, 0, 0)),
            ]
            + [pl.BlockSpec((1, tokens, width), lambda i, o: (i, 0, 0))] * len(more[:1])
            + [pl.BlockSpec((tokens, width), lambda i, o: (0, 0))] * len(more[1:3])
            + [pl.BlockSpec((tokens, width), lambda i, o: (0, group))] * len(more[3:]),
            out_specs=out_specs,
            scratch_shapes=[pltpu.VMEM((2 * SLOTS, width), jnp.bfloat16)],
        ),
        out_shape=out_shape,
        compiler_params=pltpu.CompilerParams(vmem_limit_bytes=VMEM),
        cost_estimate=pl.CostEstimate(
            flops=count * 2 * tokens * 2 * SLOTS * (width + 256),
            bytes_accessed=count * (tokens * width + 2 * SLOTS * width + tokens * lanes) * 2,
            transcendentals=0,
        ),
        name="combine",
    )(spots, routes, spread, turn, mine, theirs, *more)


def wide(value):
    return value.astype(jnp.float32)


def with_squares(values, squares):
    high = squares.astype(jnp.bfloat16)
    low = (squares - wide(high)).astype(jnp.bfloat16)
    lane = lax.broadcasted_iota(jnp.int32, (squares.shape[0], 128), 1)
    pieces = jnp.where(lane == 0, wide(high), jnp.where(lane == 1, wide(low), 0.0))
    return jnp.concatenate([values.astype(jnp.bfloat16), pieces.astype(jnp.bfloat16)], axis=1)


def finish_kernel(
    place_ref, left_base_ref, right_base_ref, left_ref, right_ref, gain_ref, down_ref, stream_ref, *rest
):
    parts, scaled, sums = rest[:4], rest[4], rest[5]
    rows = parts[0].shape[0]
    step = pl.program_id(0)
    block = down_ref.shape[0]

    @pl.when(step == 0)
    def _():
        for i in range(4):
            here = slice(i * rows, (i + 1) * rows)
            left = (left_base_ref[here] + wide(left_ref[here])).astype(jnp.bfloat16)
            right = (right_base_ref[here] + wide(right_ref[here])).astype(jnp.bfloat16)
            stream = jnp.concatenate([left, right], axis=1)
            stream_ref[here] = stream
            stream = wide(stream)
            squares = jnp.sum(stream * stream, axis=1, keepdims=True)
            nothing = jnp.zeros((rows, 128), jnp.float32)
            rank = 2 * jnp.where(place_ref[0] == i // 2, 0, 1) + jnp.where(place_ref[1] == i % 2, 0, 1)
            spot = pl.ds(pl.multiple_of(rank * rows, rows), rows)
            scaled[spot, :] = (stream * gain_ref[...]).astype(jnp.bfloat16)
            sums[spot, :] = with_squares(nothing, squares)[:, 128:]
        for i in range(4):
            parts[i][:, QL:] = sums[i * rows : (i + 1) * rows]

    value = lax.dot_general(
        scaled[...], down_ref[...], (((1,), (1,)), ((), ())), preferred_element_type=jnp.float32
    ).astype(jnp.bfloat16)
    lanes = pl.ds(pl.multiple_of(step * block, block), block)
    for i in range(4):
        parts[i][:, lanes] = value[i * rows : (i + 1) * rows]


def finish(place, bases, left, right, gain, down):
    tokens, columns = left.shape[0], gain.shape[1]
    rows = tokens // 4
    block = QL // 3
    whole = lambda *shape: pl.BlockSpec(shape, lambda n, p: (0, 0))
    return pl.pallas_call(
        finish_kernel,
        grid_spec=pltpu.PrefetchScalarGridSpec(
            num_scalar_prefetch=1,
            grid=(QL // block,),
            in_specs=[
                whole(tokens, columns // 2),
                whole(tokens, columns // 2),
                whole(tokens, columns // 2),
                whole(tokens, columns // 2),
                whole(1, columns),
                pl.BlockSpec((block, columns), lambda n, p: (n, 0)),
            ],
            out_specs=[whole(tokens, columns)] + [whole(rows, QL + 128)] * 4,
            scratch_shapes=[
                pltpu.VMEM((tokens, columns), jnp.bfloat16),
                pltpu.VMEM((tokens, 128), jnp.bfloat16),
            ],
        ),
        out_shape=[jax.ShapeDtypeStruct((tokens, columns), jnp.bfloat16)]
        + [jax.ShapeDtypeStruct((rows, QL + 128), jnp.bfloat16)] * 4,
        compiler_params=pltpu.CompilerParams(vmem_limit_bytes=VMEM),
        cost_estimate=pl.CostEstimate(
            flops=2 * tokens * columns * QL,
            bytes_accessed=2 * columns * QL + 10 * tokens * columns,
            transcendentals=0,
        ),
        name="finish",
    )(place, *bases, left, right, gain, down)


def compress_kernel(*refs):
    gain_ref, out_ref = refs[-2:]
    latent = sum(wide(ref[:, :QL]) for ref in refs[:-2])
    squares = sum(wide(ref[:, QL : QL + 1]) + wide(ref[:, QL + 1 : QL + 2]) for ref in refs[:-2])
    latent = latent * lax.rsqrt(squares / D + EPSILON)
    scale = lax.rsqrt(jnp.sum(latent * latent, axis=1, keepdims=True) / QL + EPSILON)
    out_ref[...] = with_squares(latent * scale * gain_ref[...], squares)


def compress(parts, gain):
    whole = pl.BlockSpec(memory_space=pltpu.VMEM)
    rows, lanes = parts[0].shape
    return pl.pallas_call(
        compress_kernel,
        in_specs=[whole] * (len(parts) + 1),
        out_specs=whole,
        out_shape=jax.ShapeDtypeStruct((rows, lanes), jnp.bfloat16),
        compiler_params=pltpu.CompilerParams(vmem_limit_bytes=VMEM),
        cost_estimate=pl.CostEstimate(flops=8 * rows * lanes, bytes_accessed=10 * rows * lanes, transcendentals=rows),
        name="compress",
    )(*parts, gain)


def lift_kernel(half_ref, x_ref, weight_ref, stream_ref, gain_ref, *rest):
    queries_ref, normed_ref = rest[-2:]

    @pl.when(pl.program_id(0) == 0)
    def _():
        squares = wide(x_ref[:, QL : QL + 1]) + wide(x_ref[:, QL + 1 : QL + 2])
        scale = lax.rsqrt(squares / D + EPSILON)
        normed_ref[...] = (wide(stream_ref[...]) * scale * gain_ref[...]).astype(jnp.bfloat16)

    value = jnp.dot(x_ref[:, :QL], weight_ref[...], preferred_element_type=jnp.float32)
    queries_ref[...] = value.astype(jnp.bfloat16)


def lift(half, x, weights, stream, gain, before=()):
    count, lanes = x.shape
    depth, columns = weights.shape
    tokens, width = stream.shape
    block = columns // 2
    row = pl.BlockSpec((count, width), lambda n, h: (h[0], 0))
    return pl.pallas_call(
        lift_kernel,
        grid_spec=pltpu.PrefetchScalarGridSpec(
            num_scalar_prefetch=1,
            grid=(columns // block,),
            in_specs=[
                pl.BlockSpec((count, lanes), lambda n, h: (0, 0)),
                pl.BlockSpec((depth, block), lambda n, h: (0, n)),
                row,
                pl.BlockSpec((1, width), lambda n, h: (0, 0)),
            ]
            + [pl.BlockSpec(memory_space=pl.ANY)] * len(before),
            out_specs=[pl.BlockSpec((count, block), lambda n, h: (h[0], n)), row],
        ),
        out_shape=[
            jax.ShapeDtypeStruct((tokens, columns), jnp.bfloat16),
            jax.ShapeDtypeStruct((tokens, width), jnp.bfloat16),
        ],
        input_output_aliases={5: 0, 6: 1} if before else {},
        compiler_params=pltpu.CompilerParams(vmem_limit_bytes=VMEM),
        cost_estimate=pl.CostEstimate(
            flops=2 * count * depth * columns,
            bytes_accessed=2 * depth * columns + 2 * count * columns,
            transcendentals=0,
        ),
        name="lift",
    )(half, x, weights, stream, gain, *before)


def shards(expert_out, expert_ids, gate_levels, residual, attn_gain, wq_a, latent_gain, wq_b):
    half = lax.axis_index("dp")
    place = lax.axis_index("expert")
    quarter = jnp.asarray(QUARTERS)[half, lax.axis_index("tensor")]
    upper, odd = quarter // 2, quarter % 2
    tokens = expert_ids.shape[0]
    columns = residual.shape[1]
    width = columns // GROUPS

    part = wq_b.shape[0] // 2

    def spread_out(value):
        return lax.all_gather(value, ("dp", "expert"), axis=0, tiled=True)

    down = spread_out(lax.dynamic_slice_in_dim(wq_a.T, half * part, part, 0))
    up_part = lax.dynamic_slice_in_dim(wq_b, half * part, part, 0)
    gain = latent_gain.reshape(RING, 2, part).transpose(1, 0, 2).reshape(1, QL)

    owners = jnp.asarray(owner_table())[half, place]
    spots = jnp.asarray(spot_table())[half, place]
    holders = jnp.asarray(holder_table())[half, place]
    experts = (holders[:, None] * HOLD + jnp.arange(HOLD, dtype=jnp.int32)[None, :]).reshape(-1)
    experts = jnp.concatenate([experts, jnp.full((64 - experts.shape[0],), -1, jnp.int32)])
    experts = jnp.broadcast_to(experts.astype(jnp.float32)[:, None], (64, tokens))

    packed = [jnp.concatenate([expert_ids.T, gate_levels.T], axis=0)]

    def double(kind, beside=()):
        received = lax.ppermute(packed[-1], "expert", [(e, partner(kind, e)) for e in range(RING)])
        received, *_ = lax.optimization_barrier((received, *beside))
        packed.append(jnp.concatenate([packed[-1], received], axis=0))

    double(ORDERS[0][0])
    double(ORDERS[0][1])
    spot = jnp.arange(RING * RING, dtype=jnp.int32)
    slots = expert_out.transpose(0, 2, 1, 3).reshape(SLOTS, RING, columns)
    relayed, first = [], []
    for g in range(GROUPS):
        source = (spot % RING) * RING + jnp.repeat(owners[g], RING)
        move = (source[:, None] == spot[None, :]).astype(jnp.bfloat16)
        move, _ = lax.optimization_barrier((move, packed[2 + g]))
        relayed.append(relay(slots, move, g))
        double(ORDERS[0][2 + g], relayed[g][:1])
        left, right, _ = lax.optimization_barrier((relayed[g][0], relayed[g][1], packed[2 * g + 2]))
        first.append([swap(left, g, 0), swap(right, g, 0)])

    position = jnp.arange(tokens, dtype=jnp.int32)
    later = (position[:, None] < position[None, :]).astype(jnp.bfloat16)
    routes = route(packed[-1].reshape(RING, 16, tokens), experts, later, tokens)
    slot = np.arange(SLOTS)
    turn = np.broadcast_to(STEP * np.tile(slot % CAP, 2)[None, :], (8, 2 * SLOTS))
    turn = jnp.asarray(turn.astype(np.float32))
    lanes = np.arange(64)[:, None]
    spread = []
    for g in range(GROUPS):
        expert = (slot // CAP)[None, :]
        hit = np.concatenate([lanes == expert, lanes == expert + HOLD * (g + 1)], axis=1)
        spread.append(jnp.asarray(np.concatenate([hit, STEP * hit], axis=0).astype(np.float32)).astype(jnp.bfloat16))

    def summed(g, start, more=(), group=None):
        received = first[g][start // 4]
        return combine(spots[g], routes, spread[g], turn, relayed[g][2], received, start, 2, tokens, more, group)

    groups = range(GROUPS)
    passed = [[summed(g, 2 * i) for g in groups] for i in range(2)]
    second_a = [swap(passed[0][g], g, 1) for g in groups]
    second_b = [swap(passed[1][g], g, 1) for g in groups]
    kept_a = [summed(g, 4, (second_a[g],)) for g in groups]
    third_a = [swap(kept_a[g][0], g, 2) for g in groups]
    third_b = [swap(kept_a[g][1], g, 2) for g in groups]
    last, base = zip(
        *[summed(g, 6, (second_b[g], third_a[g], third_b[g], residual), g) for g in groups], strict=True
    )
    fourth = [swap(last[g], g, 3) for g in groups]
    up_part, _ = lax.optimization_barrier((up_part, last[-1]))
    up = spread_out(up_part)

    here = upper.reshape(1)
    there = 1 - here
    wide_gain = attn_gain.reshape(1, columns)
    count = lax.axis_size("tensor")
    across = [(y, (y + 2) % count) for y in range(count)]
    place_here = jnp.stack([upper, odd])
    stream, own, beside, near, far = finish(place_here, base, *fourth, wide_gain, down)
    far = lax.ppermute(far, "tensor", across)
    near = turn_to(near, 0)
    normed_mine = compress((own, turn_to(beside, 1), near, far), gain)
    normed_theirs = turn_to(normed_mine, 1)
    half_here = jnp.where(
        odd == 0,
        jnp.concatenate([normed_mine, normed_theirs], axis=0),
        jnp.concatenate([normed_theirs, normed_mine], axis=0),
    )
    half_there = turn_to(half_here, 0)
    queries, normed = lift(here, half_here, up, stream, wide_gain)
    queries, normed = lift(there, half_there, up, stream, wide_gain, (queries, normed))
    return (stream, normed, queries)


def solution(mesh):
    return jax.shard_map(
        shards,
        mesh=mesh,
        in_specs=(
            P(("dp", "expert"), None, None, "tensor"),
            P(("dp", "expert"), None),
            P(("dp", "expert"), None),
            P(("dp", "expert"), "tensor"),
            P("tensor"),
            P("tensor", "expert"),
            P(),
            P("expert", "tensor"),
        ),
        out_specs=(
            P(("dp", "expert"), "tensor"),
            P(("dp", "expert"), "tensor"),
            P(("dp", "expert"), "tensor"),
        ),
        check_vma=False,
    )
```
